256 devices in a mesh: row: 32 (over z, y), col: 8 (over x, core).
Axes of the slice: x: 4, y: 4, z: 8, core: 2. Of those that a mesh axis runs over, the one named last changes fastest.
Arguments:
- jacobian: float32 [512, 16384], P('col', 'row'), may hold values from -0.25 to 0.25
- residual: float32 [512], P('col'), may hold values from -240 to 240
- normal_prior: float32 [16384, 16384], P('row', 'col'), may hold values from -0.3 to 0.3
Outputs:
- normal_damped: float32 [16384, 16384], P('row', 'col')
- gradient: float32 [16384], P('row')
The draws below stay inside these ranges and needn't reach their ends.
All inputs are finite; a program needn't handle non-finite values.
Results may differ from the reference program's by a relative error of at most 0.00008.
Values sent between devices are 32-bit elements; how exact they have to be, the bound alone decides.
No kernel may reach another device: no remote copies, remote signals or barrier semaphores. Data moves between devices by JAX's collectives and lax.ppermute only.
A program may use at most 64 MiB of HBM per device.

```python
import math
import jax
import jax.numpy as jnp
from jax import lax

N = 16384
M = 512


def draw_residual(key, part):
    key = jax.random.fold_in(key, 5)
    key_spread, key_base = jax.random.split(key)
    position = jnp.arange(M, dtype=jnp.float32) / M
    spread = jnp.exp(jax.random.uniform(key_spread, (M,), jnp.float32, 0.0, math.log(10.0)))
    base = jnp.clip(jax.random.normal(key_base, (M,), jnp.float32), -4.0, 4.0)
    trend = jnp.exp(math.log(3.0) * position)
    return (base * spread * trend).astype(jnp.float32)


def block_levels(stream_key, shape, pieces, least, top_value):
    gain, own = 1.0, jax.random.fold_in(stream_key, 6)
    for dim, blocks in pieces:
        draws = jnp.exp(jax.random.uniform(jax.random.fold_in(own, dim), (blocks,), jnp.float32, least / len(pieces), top_value / len(pieces)))
        gain = gain * jnp.repeat(draws, shape[dim] // blocks).reshape([-1 if axis == dim else 1 for axis in range(len(shape))])
    return gain


def centred(stream_key, extent, deviation, limit, pieces=(), kind=jnp.bfloat16):
    loudness = block_levels(stream_key, extent, pieces, -0.22, 0.18) if pieces else 1.0
    array = jax.random.normal(stream_key, extent, jnp.float32) * deviation * loudness
    return jnp.minimum(jnp.maximum(array, -limit), limit).astype(kind)


def setup_inputs(seed: int = 0) -> dict:
    arg_keys = jax.random.split(jax.random.key(seed), 4)
    return {
        "jacobian": centred(arg_keys[0], (M, N), M ** -0.5, 0.25, ((0, 8), (1, 32)), jnp.float32),
        "residual": draw_residual(jax.random.fold_in(arg_keys[3], 71), 0),
        "normal_prior": centred(arg_keys[2], (N, N), 0.05, 0.3, ((0, 32), (1, 8)), jnp.float32),
    }


damping_scale = 0.2

def reference(jacobian, residual, normal_prior):
    highest = lax.Precision.HIGHEST
    cross = jnp.dot(jacobian.T, jacobian, preferred_element_type=jnp.float32, precision=highest)
    gradient = jnp.dot(residual, jacobian, preferred_element_type=jnp.float32, precision=highest)
    damping = damping_scale * jnp.sqrt(jnp.sum(residual * residual) / M + 1e-06)
    positions = jnp.arange(N)
    cross = cross.at[positions, positions].multiply(1.0 + damping)
    return (normal_prior + cross, gradient)
```

```python
import functools

import jax
import jax.numpy as jnp
from jax import lax
from jax.experimental import pallas as pl
from jax.experimental.pallas import tpu as pltpu
from jax.sharding import PartitionSpec as P

damping_scale = 0.2
Z, Y, X, K = 8, 4, 4, 2
BLOCK = 512
ROWS = 64
PACK = ROWS + 8
VMEM = 16 * 1024 * 1024

SHIFT = (0, 4, 1, 7, 2, 6, 3, 5)
ALONG = (0, 2, 6, 1, 3, 7, 5, 4)


def place(z, y, x, k):
    return ((z % Z) * Y + y % Y) * X * K + (x % X) * K + k


def permute(array, where):
    pairs = [
        (place(z, y, x, k), place(*where(z, y, x, k)))
        for z in range(Z)
        for y in range(Y)
        for x in range(X)
        for k in range(K)
    ]
    return lax.ppermute(array, ("row", "col"), pairs)


def fetch(array, z=0, y=0):
    return permute(array, lambda z0, y0, x, k: (z0 - z, y0 - y, x, k))


def swap(array, x=0, k=0):
    return permute(array, lambda z, y, x0, k0: (z, y, x0 ^ x, k0 ^ k))


def spread(array):
    return permute(array, lambda z, y, x, k: (z + SHIFT[x * K + k], y, z // K, z % K))


def join(*arrays):
    return jnp.concatenate(arrays, axis=0)


def block_of(shift):
    return jnp.where(shift < 4, 2 * shift, (2 * (Z - shift) + 1) % Z)


def split(array):
    top = array.astype(jnp.bfloat16)
    return top, (array - top.astype(jnp.float32)).astype(jnp.bfloat16)


def panel_kernel(where, panel, high, low, gradient, damping, ordered):
    col_index = where[1]
    total = jnp.zeros((8, BLOCK), jnp.float32)
    squares = jnp.zeros((8, ROWS), jnp.float32)
    for d, along in enumerate(ALONG):
        block = block_of((where[2] + (along + Z) - col_index) % Z)
        apart = block ^ col_index
        start = pl.multiple_of((apart // K + X * (apart % K)) * PACK, 8)
        rows = panel[pl.ds(start, ROWS), :]
        residual = panel[pl.ds(start + ROWS, 8), :][:, :ROWS]
        squares += residual * residual
        total += lax.dot_general(
            residual,
            rows,
            (((1,), (0,)), ((), ())),
            precision=lax.Precision.HIGHEST,
            preferred_element_type=jnp.float32,
        )
        ordered[d * ROWS : (d + 1) * ROWS, :] = rows
    gradient[...] = jnp.sum(total, axis=0, keepdims=True)
    mean = jnp.sum(squares, keepdims=True) / (ROWS * X * K)
    damping[...] = jnp.broadcast_to(damping_scale * jnp.sqrt(mean + 1e-06), damping.shape)
    high[...], low[...] = split(ordered[...].T)


def times(a, b):
    return lax.dot_general(
        a, b, (((1,), (0,)), ((), ())), preferred_element_type=jnp.float32
    )


def cross_kernel(where, *refs, counts, diagonal):
    pieces = refs[: sum(counts)]
    high, low, damping, prior = refs[sum(counts) :][:4]
    out, top, rest = refs[-3:]
    step = pl.program_id(0)
    first = 0
    for i, count in enumerate(counts):
        mine = pieces[first : first + count]
        first += count

        @pl.when(step == i)
        def _():
            at = 0
            for piece in mine:
                end = at + piece.shape[0]
                top[at:end, :], rest[at:end, :] = split(piece[...])
                at = end

    cross = times(high[...], top[...])
    cross += times(high[...], rest[...]) + times(low[...], top[...])
    if diagonal:
        row = lax.broadcasted_iota(jnp.int32, cross.shape, 0)
        col = lax.broadcasted_iota(jnp.int32, cross.shape, 1)
        marked = (row == col) & (step == 0) & (where[1] == where[2])
        cross = cross * jnp.where(marked, 1.0 + damping[0:1, 0:1], 1.0)
    out[...] = prior[...] + cross


def full(shape):
    return pl.BlockSpec(shape, lambda i, w: (0, 0))


def kernel(body, grid, in_specs, out_specs, out_shape, name, scratch=(), aliases=None):
    return pl.pallas_call(
        body,
        grid_spec=pltpu.PrefetchScalarGridSpec(
            num_scalar_prefetch=1,
            grid=grid,
            in_specs=in_specs,
            out_specs=out_specs,
            scratch_shapes=scratch,
        ),
        out_shape=out_shape,
        input_output_aliases=aliases or {},
        compiler_params=pltpu.CompilerParams(vmem_limit_bytes=VMEM),
        cost_estimate=pl.CostEstimate(flops=1000, bytes_accessed=1000, transcendentals=0),
        name=name,
    )


def per_device(jacobian, residual, normal_prior):
    row_index, col_index = lax.axis_index("row"), lax.axis_index("col")
    where = jnp.stack([row_index % Y, col_index, row_index // Y]).astype(jnp.int32)

    together = lax.optimization_barrier
    shard = spread(jacobian)
    tail = jnp.zeros((8, BLOCK), jnp.float32).at[0, :ROWS].set(residual)
    own = join(jacobian, tail)
    own = join(own, swap(own, x=1))

    up, down = fetch(shard, z=2), fetch(shard, z=-2)
    far = fetch(shard, y=2)
    own = join(own, swap(own, x=2))
    up, down, far = together((up, down, far))
    ups, downs = fetch(join(shard, up), z=1), fetch(join(shard, down), z=-1)
    across = fetch(up, z=2)
    up_far, down_far = fetch(far, z=2), fetch(far, z=-2)
    own = join(own, swap(own, k=1))
    column = [join(shard, up, down), join(ups, downs, across)]
    column_near = [fetch(part, y=1) for part in column]
    column_back = [fetch(part, y=3) for part in column]
    ups_far, downs_far = fetch(join(far, up_far), z=1), fetch(join(far, down_far), z=-1)
    across_far = fetch(down_far, z=-2)
    column_far = [far, up_far, down_far, ups_far, downs_far, across_far]

    half = jax.ShapeDtypeStruct((BLOCK, BLOCK), jnp.bfloat16)
    outs = [half, half, jax.ShapeDtypeStruct((1, BLOCK), jnp.float32)]
    outs += [jax.ShapeDtypeStruct((8, 128), jnp.float32)]
    high, low, gradient, damping = kernel(
        panel_kernel,
        (1,),
        [full(own.shape)],
        [full(s.shape) for s in outs],
        outs,
        "own_panel",
        [pltpu.VMEM((BLOCK, BLOCK), jnp.float32)],
    )(where, own)

    def cross(columns, first, before=()):
        block = pl.BlockSpec((BLOCK, BLOCK), lambda i, w: (0, (2 * i + first + w[0]) % Y))
        pieces = [piece for column in columns for piece in column]
        counts = tuple(len(column) for column in columns)
        return kernel(
            functools.partial(cross_kernel, counts=counts, diagonal=first == 0),
            (len(columns),),
            [full(piece.shape) for piece in pieces]
            + [full(high.shape)] * 2
            + [full(damping.shape), block]
            + [pl.BlockSpec(memory_space=pl.ANY)] * len(before),
            block,
            jax.ShapeDtypeStruct(normal_prior.shape, jnp.float32),
            f"cross_{first}",
            [pltpu.VMEM((BLOCK, BLOCK), jnp.bfloat16)] * 2,
            {len(pieces) + 5: 0} if before else None,
        )(where, *pieces, high, low, damping, normal_prior, *before)

    normal = cross([column, column_far], 0)
    normal = cross([column_near, column_back], 1, (normal,))
    return normal, gradient.reshape(BLOCK)


def solution(mesh):
    return jax.shard_map(
        per_device,
        mesh=mesh,
        in_specs=(P("col", "row"), P("col"), P("row", "col")),
        out_specs=(P("row", "col"), P("row")),
        check_vma=False,
    )
```

```python
import functools

import jax
import jax.numpy as jnp
from jax import lax
from jax.experimental import pallas as pl
from jax.experimental.pallas import tpu as pltpu
from jax.sharding import PartitionSpec as P

damping_scale = 0.2
Z, Y, X, K = 8, 4, 4, 2
BLOCK = 512
ROWS = 64
PACK = ROWS + 8
VMEM = 16 * 1024 * 1024

SHIFT = (0, 4, 1, 7, 2, 6, 3, 5)
ALONG = (0, 2, 6, 1, 3, 7, 5, 4)


def place(z, y, x, k):
    return ((z % Z) * Y + y % Y) * X * K + (x % X) * K + k


def permute(array, where):
    pairs = [
        (place(z, y, x, k), place(*where(z, y, x, k)))
        for z in range(Z)
        for y in range(Y)
        for x in range(X)
        for k in range(K)
    ]
    return lax.ppermute(array, ("row", "col"), pairs)


def fetch(array, z=0, y=0):
    return permute(array, lambda z0, y0, x, k: (z0 - z, y0 - y, x, k))


def swap(array, x=0, k=0):
    return permute(array, lambda z, y, x0, k0: (z, y, x0 ^ x, k0 ^ k))


def spread(array, y=0):
    return permute(array, lambda z, y0, x, k: (z + SHIFT[x * K + k], y0 - y, z // K, z % K))


def join(*arrays):
    return jnp.concatenate(arrays, axis=0)


def block_of(shift):
    return jnp.where(shift < 4, 2 * shift, (2 * (Z - shift) + 1) % Z)


def split(array):
    top = array.astype(jnp.bfloat16)
    return top, (array - top.astype(jnp.float32)).astype(jnp.bfloat16)


def panel_kernel(where, panel, both, gradient, damping, ordered):
    col_index = where[1]
    total = jnp.zeros((8, BLOCK), jnp.float32)
    squares = jnp.zeros((8, ROWS), jnp.float32)
    for d, along in enumerate(ALONG):
        block = block_of((where[2] + (along + Z) - col_index) % Z)
        apart = block ^ col_index
        start = pl.multiple_of((apart // K + X * (apart % K)) * PACK, 8)
        rows = panel[pl.ds(start, ROWS), :]
        residual = panel[pl.ds(start + ROWS, 8), :][:, :ROWS]
        squares += residual * residual
        total += lax.dot_general(
            residual,
            rows,
            (((1,), (0,)), ((), ())),
            precision=lax.Precision.HIGHEST,
            preferred_element_type=jnp.float32,
        )
        ordered[d * ROWS : (d + 1) * ROWS, :] = rows
    gradient[...] = jnp.sum(total, axis=0, keepdims=True)
    mean = jnp.sum(squares, keepdims=True) / (ROWS * X * K)
    damping[...] = jnp.broadcast_to(damping_scale * jnp.sqrt(mean + 1e-06), damping.shape)
    high, low = split(ordered[...].T)
    both[:, :BLOCK] = high
    both[:, BLOCK : 2 * BLOCK] = high
    both[:, 2 * BLOCK :] = low


def times(a, b):
    return lax.dot_general(
        a, b, (((1,), (0,)), ((), ())), preferred_element_type=jnp.float32
    )


def cross_kernel(where, *refs, counts, which, diagonal):
    pieces = refs[: sum(counts)]
    both, damping, prior = refs[sum(counts) :][:3]
    out, column = refs[-2:]
    step = pl.program_id(0)
    place = (which(step) + where[0]) % Y * BLOCK
    first = 0
    for i, count in enumerate(counts):
        mine = pieces[first : first + count]
        first += count

        @pl.when(step == i)
        def _():
            at = 0
            for piece in mine:
                end = at + piece.shape[0]
                high, low = split(piece[...])
                column[at:end, :] = high
                column[BLOCK + at : BLOCK + end, :] = low
                column[2 * BLOCK + at : 2 * BLOCK + end, :] = high
                at = end

    cross = times(both[...], column[...])
    if diagonal:
        row = lax.broadcasted_iota(jnp.int32, cross.shape, 0)
        col = lax.broadcasted_iota(jnp.int32, cross.shape, 1)
        marked = (row == col) & (where[1] == where[2])
        cross = cross * jnp.where(marked, 1.0 + damping[0:1, 0:1], 1.0)
    out[...] = prior[:, pl.ds(pl.multiple_of(place, BLOCK), BLOCK)] + cross


held = pl.BlockSpec(memory_space=pltpu.VMEM)


def kernel(body, grid, in_specs, out_specs, out_shape, name, scratch=(), aliases=None):
    return pl.pallas_call(
        body,
        grid_spec=pltpu.PrefetchScalarGridSpec(
            num_scalar_prefetch=1,
            grid=grid,
            in_specs=in_specs,
            out_specs=out_specs,
            scratch_shapes=scratch,
        ),
        out_shape=out_shape,
        input_output_aliases=aliases or {},
        compiler_params=pltpu.CompilerParams(vmem_limit_bytes=VMEM),
        cost_estimate=pl.CostEstimate(flops=1000, bytes_accessed=1000, transcendentals=0),
        name=name,
    )


def per_device(jacobian, residual, normal_prior):
    row_index, col_index = lax.axis_index("row"), lax.axis_index("col")
    where = jnp.stack([row_index % Y, col_index, row_index // Y]).astype(jnp.int32)

    together = lax.optimization_barrier
    shard, far = spread(jacobian), spread(jacobian, y=2)
    tail = jnp.zeros((8, BLOCK), jnp.float32).at[0, :ROWS].set(residual)
    shard, own = together((shard, join(jacobian, tail)))

    up, down = fetch(shard, z=2), fetch(shard, z=-2)
    own = join(own, swap(own, x=1))
    up, down = together((up, down))
    ups, downs = fetch(join(shard, up), z=1), fetch(join(shard, down), z=-1)
    across = fetch(up, z=2)
    up_far, down_far = fetch(far, z=2), fetch(far, z=-2)
    first = join(shard, up, down)
    near, back = fetch(first, y=1), fetch(first, y=3)
    up_far, down_far, near, back, ups, downs, across = together(
        (up_far, down_far, near, back, ups, downs, across)
    )
    own = join(own, swap(own, x=2))
    own = join(own, swap(own, k=1))
    rest = join(ups, downs, across)
    near_rest, back_rest = fetch(rest, y=1), fetch(rest, y=3)
    ups_far, downs_far = fetch(join(far, up_far), z=1), fetch(join(far, down_far), z=-1)
    across_far = fetch(down_far, z=-2)
    columns = [
        [first, rest],
        [near, near_rest],
        [far, up_far, down_far, ups_far, downs_far, across_far],
        [back, back_rest],
    ]

    outs = [
        jax.ShapeDtypeStruct((BLOCK, 3 * BLOCK), jnp.bfloat16),
        jax.ShapeDtypeStruct((1, BLOCK), jnp.float32),
        jax.ShapeDtypeStruct((8, 128), jnp.float32),
    ]
    both, gradient, damping = kernel(
        panel_kernel,
        (),
        [held],
        [held] * len(outs),
        outs,
        "own_panel",
        [pltpu.VMEM((BLOCK, BLOCK), jnp.float32)],
    )(where, own)

    def cross(chosen, before=()):
        which = lambda i: sum(dy * (i == at) for at, dy in enumerate(chosen))
        block = pl.BlockSpec((BLOCK, BLOCK), lambda i, w: (0, (which(i) + w[0]) % Y))
        pieces = [piece for dy in chosen for piece in columns[dy]]
        counts = tuple(len(columns[dy]) for dy in chosen)
        return kernel(
            functools.partial(cross_kernel, counts=counts, which=which, diagonal=chosen == (0,)),
            (len(chosen),),
            [held] * (len(pieces) + 3)
            + [pl.BlockSpec(memory_space=pl.ANY)] * len(before),
            block,
            jax.ShapeDtypeStruct(normal_prior.shape, jnp.float32),
            "cross_" + "_".join(map(str, chosen)),
            [pltpu.VMEM((3 * BLOCK, BLOCK), jnp.bfloat16)],
            {len(pieces) + 4: 0} if before else None,
        )(where, *pieces, both, damping, normal_prior, *before)

    normal = cross((0,))
    normal = cross((1, 3, 2), (normal,))
    return normal, gradient.reshape(BLOCK)


def solution(mesh):
    return jax.shard_map(
        per_device,
        mesh=mesh,
        in_specs=(P("col", "row"), P("col"), P("row", "col")),
        out_specs=(P("row", "col"), P("row")),
        check_vma=False,
    )
```

```python
import functools

import jax
import jax.numpy as jnp
from jax import lax
from jax.experimental import pallas as pl
from jax.experimental.pallas import tpu as pltpu
from jax.sharding import PartitionSpec as P

damping_scale = 0.2
Z, Y, X, K = 8, 4, 4, 2
BLOCK = 512
ROWS = 64
PACK = ROWS + 8
VMEM = 16 * 1024 * 1024

SHIFT = (0, 4, 1, 7, 2, 6, 3, 5)
ALONG = (0, 2, 6, 1, 3, 7, 5, 4)


def place(z, y, x, k):
    return ((z % Z) * Y + y % Y) * X * K + (x % X) * K + k


def permute(array, where):
    pairs = [
        (place(z, y, x, k), place(*where(z, y, x, k)))
        for z in range(Z)
        for y in range(Y)
        for x in range(X)
        for k in range(K)
    ]
    return lax.ppermute(array, ("row", "col"), pairs)


def fetch(array, z=0, y=0):
    return permute(array, lambda z0, y0, x, k: (z0 - z, y0 - y, x, k))


def swap(array, x=0, k=0):
    return permute(array, lambda z, y, x0, k0: (z, y, x0 ^ x, k0 ^ k))


def spread(array, y=0):
    return permute(array, lambda z, y0, x, k: (z + SHIFT[x * K + k], y0 - y, z // K, z % K))


def join(*arrays):
    return jnp.concatenate(arrays, axis=0)


def block_of(shift):
    return jnp.where(shift < 4, 2 * shift, (2 * (Z - shift) + 1) % Z)


def split(array):
    top = array.astype(jnp.bfloat16)
    return top, (array - top.astype(jnp.float32)).astype(jnp.bfloat16)


def panel_kernel(where, panel, both, gradient, damping, ordered):
    col_index = where[1]
    total = jnp.zeros((8, BLOCK), jnp.float32)
    squares = jnp.zeros((8, ROWS), jnp.float32)
    for d, along in enumerate(ALONG):
        block = block_of((where[2] + (along + Z) - col_index) % Z)
        apart = block ^ col_index
        start = pl.multiple_of((apart // K + X * (apart % K)) * PACK, 8)
        rows = panel[pl.ds(start, ROWS), :]
        residual = panel[pl.ds(start + ROWS, 8), :][:, :ROWS]
        squares += residual * residual
        total += lax.dot_general(
            residual,
            rows,
            (((1,), (0,)), ((), ())),
            precision=lax.Precision.HIGHEST,
            preferred_element_type=jnp.float32,
        )
        ordered[d * ROWS : (d + 1) * ROWS, :] = rows
    gradient[...] = jnp.sum(total, axis=0, keepdims=True)
    mean = jnp.sum(squares, keepdims=True) / (ROWS * X * K)
    damping[...] = jnp.broadcast_to(damping_scale * jnp.sqrt(mean + 1e-06), damping.shape)
    high, low = split(ordered[...].T)
    both[:, :BLOCK] = high
    both[:, BLOCK : 2 * BLOCK] = high
    both[:, 2 * BLOCK :] = low


def times(a, b):
    return lax.dot_general(
        a, b, (((1,), (0,)), ((), ())), preferred_element_type=jnp.float32
    )


def cross_kernel(where, *refs, counts, which, diagonal):
    pieces = refs[: sum(counts)]
    both, damping, prior = refs[sum(counts) :][:3]
    out, column = refs[-2:]
    step = pl.program_id(0)
    place = (which(step) + where[0]) % Y * BLOCK
    first = 0
    for i, count in enumerate(counts):
        mine = pieces[first : first + count]
        first += count

        @pl.when(step == i)
        def _():
            at = 0
            for piece in mine:
                end = at + piece.shape[0]
                high, low = split(piece[...])
                column[at:end, :] = high
                column[BLOCK + at : BLOCK + end, :] = low
                column[2 * BLOCK + at : 2 * BLOCK + end, :] = high
                at = end

    cross = times(both[...], column[...])
    if diagonal:
        row = lax.broadcasted_iota(jnp.int32, cross.shape, 0)
        col = lax.broadcasted_iota(jnp.int32, cross.shape, 1)
        marked = (row == col) & (where[1] == where[2])
        cross = cross * jnp.where(marked, 1.0 + damping[0:1, 0:1], 1.0)
    out[...] = prior[:, pl.ds(pl.multiple_of(place, BLOCK), BLOCK)] + cross


held = pl.BlockSpec(memory_space=pltpu.VMEM)


def kernel(body, grid, in_specs, out_specs, out_shape, name, scratch=(), aliases=None):
    return pl.pallas_call(
        body,
        grid_spec=pltpu.PrefetchScalarGridSpec(
            num_scalar_prefetch=1,
            grid=grid,
            in_specs=in_specs,
            out_specs=out_specs,
            scratch_shapes=scratch,
        ),
        out_shape=out_shape,
        input_output_aliases=aliases or {},
        compiler_params=pltpu.CompilerParams(vmem_limit_bytes=VMEM),
        cost_estimate=pl.CostEstimate(flops=1000, bytes_accessed=1000, transcendentals=0),
        name=name,
    )


def per_device(jacobian, residual, normal_prior):
    row_index, col_index = lax.axis_index("row"), lax.axis_index("col")
    where = jnp.stack([row_index % Y, col_index, row_index // Y]).astype(jnp.int32)

    together = lax.optimization_barrier
    shard, far = spread(jacobian), spread(jacobian, y=2)
    tail = jnp.zeros((8, BLOCK), jnp.float32).at[0, :ROWS].set(residual)
    shard, own = together((shard, join(jacobian, tail)))

    up, down = fetch(shard, z=2), fetch(shard, z=-2)
    own = join(own, swap(own, x=1))
    up, down = together((up, down))
    ups, downs = fetch(join(shard, up), z=1), fetch(join(shard, down), z=-1)
    across = fetch(up, z=2)
    up_far, down_far = fetch(far, z=2), fetch(far, z=-2)
    own, up_far, down_far = together((own, up_far, down_far))
    own = join(own, swap(own, x=2))
    first = join(shard, up, down)
    near, back = fetch(first, y=1), fetch(first, y=3)
    up_far, down_far, near, back, ups, downs, across = together(
        (up_far, down_far, near, back, ups, downs, across)
    )
    own = join(own, swap(own, k=1))
    rest = join(ups, downs, across)
    near_rest, back_rest = fetch(rest, y=1), fetch(rest, y=3)
    ups_far, downs_far = fetch(join(far, up_far), z=1), fetch(join(far, down_far), z=-1)
    across_far = fetch(down_far, z=-2)
    columns = [
        [first, rest],
        [near, near_rest],
        [far, up_far, down_far, ups_far, downs_far, across_far],
        [back, back_rest],
    ]

    outs = [
        jax.ShapeDtypeStruct((BLOCK, 3 * BLOCK), jnp.bfloat16),
        jax.ShapeDtypeStruct((1, BLOCK), jnp.float32),
        jax.ShapeDtypeStruct((8, 128), jnp.float32),
    ]
    both, gradient, damping = kernel(
        panel_kernel,
        (),
        [held],
        [held] * len(outs),
        outs,
        "own_panel",
        [pltpu.VMEM((BLOCK, BLOCK), jnp.float32)],
    )(where, own)

    def cross(chosen, before=()):
        which = lambda i: sum(dy * (i == at) for at, dy in enumerate(chosen))
        block = pl.BlockSpec((BLOCK, BLOCK), lambda i, w: (0, (which(i) + w[0]) % Y))
        pieces = [piece for dy in chosen for piece in columns[dy]]
        counts = tuple(len(columns[dy]) for dy in chosen)
        return kernel(
            functools.partial(cross_kernel, counts=counts, which=which, diagonal=chosen == (0,)),
            (len(chosen),),
            [held] * (len(pieces) + 3)
            + [pl.BlockSpec(memory_space=pl.ANY)] * len(before),
            block,
            jax.ShapeDtypeStruct(normal_prior.shape, jnp.float32),
            "cross_" + "_".join(map(str, chosen)),
            [pltpu.VMEM((3 * BLOCK, BLOCK), jnp.bfloat16)],
            {len(pieces) + 4: 0} if before else None,
        )(where, *pieces, both, damping, normal_prior, *before)

    normal = cross((0,))
    normal = cross((1, 3, 2), (normal,))
    return normal, gradient.reshape(BLOCK)


def solution(mesh):
    return jax.shard_map(
        per_device,
        mesh=mesh,
        in_specs=(P("col", "row"), P("col"), P("row", "col")),
        out_specs=(P("row", "col"), P("row")),
        check_vma=False,
    )
```
